32 devices in a mesh: groups: 2 (over y), tp: 16 (over z, x, core).
Axes of the slice: x: 2, y: 2, z: 4, core: 2. Of those that a mesh axis runs over, the one named last changes fastest.
Arguments:
- hidden_in: bfloat16 [32, 8, 512], P(('groups', 'tp')), parts along dimension 0, may hold values from -6 to 6
- norm_gain: float32 [8192], replicated, may hold values from 0.1 to 1.9
- q_blocks: bfloat16 [16, 16, 128, 2048], P('tp'), may hold values from -0.0625 to 0.0625
- o_blocks: bfloat16 [16, 2048, 16, 128], P('tp'), may hold values from -1.5 to 1.5
- kv_blocks: bfloat16 [2, 1024, 8192], P(None, None, 'tp'), may hold values from -0.0625 to 0.0625
- kv_assign: int32 [16], replicated, may hold values from 0 to 7, as said below
- key_cache: bfloat16 [32, 8, 2048, 128], P(('groups', 'tp')), parts along dimension 0, may hold values from -240 to 240
- value_cache: bfloat16 [32, 8, 2048, 128], P(('groups', 'tp')), parts along dimension 0, may hold values from -6 to 6
- lengths: int32 [32, 8], P(('groups', 'tp')), parts along dimension 0, may hold values from 1 to 2048, as said below
Outputs:
- attn_out: bfloat16 [32, 8, 512], P(('groups', 'tp')), parts along dimension 0
The draws below stay inside these ranges and needn't reach their ends.
There are 2 independent parts, one for each index of `groups`. The reference program is written for one: setup_inputs(seed, part) draws one part's arguments, and reference() takes and returns one part's arrays. A program takes and returns all parts, laid end to end along the dimension named above; an argument that names none is the same for every part. Nothing has to cross between parts.
Inputs may be any that keep to these rules, and one draw needn't show every extreme that they name: `kv_assign`: entries 2m and 2m + 1 are equal, and each of the 8 key-value heads is named by exactly two entries. `lengths`: in every rank one row has all 2048 positions valid.
All inputs are finite; a program needn't handle non-finite values.
Results may differ from the reference program's by a relative error of at most 0.011.
The reference program's roundings to bfloat16 on the way count: a program that leaves them out, or rounds other values in their place, can miss the bound.
Values may be sent and summed in bfloat16 or wider, within the bound.
A program may use at most 128 MiB of HBM per device.

```python
import jax
import jax.numpy as jnp
from jax import lax

D = 8192
QH = 64
KVH = 8
HD = 128
ROLL = 16
ROWS = 8
RANKS = 16
GR = 4
QG = 16
GC = 4
DS = 512
CTXH = 2048


def draw_kv_assign(key, part):
    order = jax.random.permutation(jax.random.fold_in(key, 11), KVH)
    return jnp.repeat(order, 2).astype(jnp.int32)


def draw_lengths(key, part):
    base = jax.random.randint(jax.random.fold_in(key, 21), (RANKS, ROWS), 1, CTXH + 1)
    chosen = jax.random.randint(jax.random.fold_in(key, 22), (RANKS, 1), 0, ROWS)
    positions = jnp.arange(ROWS, dtype=jnp.int32)[None, :]
    return jnp.where(positions == chosen, CTXH, base).astype(jnp.int32)


def draw_key_cache(key, part):
    base = jnp.clip(jax.random.normal(jax.random.fold_in(key, 31), (RANKS, ROWS, CTXH, HD), jnp.float32), -6.0, 6.0)
    return base.astype(jnp.bfloat16)


def levels(rng, dims, shards, least, high):
    factor_of, own = 1.0, jax.random.fold_in(rng, 6)
    for dim, blocks in shards:
        steps = jnp.exp(jax.random.uniform(jax.random.fold_in(own, dim), (blocks,), jnp.float32, least / len(shards), high / len(shards)))
        factor_of = factor_of * jnp.repeat(steps, dims[dim] // blocks).reshape([-1 if axis == dim else 1 for axis in range(len(dims))])
    return factor_of


def noise(key, dims, width, reach, split=(), kind=jnp.bfloat16):
    array = width * jax.random.normal(key, dims, jnp.float32)
    if split:
        array = array * levels(key, dims, split, -0.22, 0.18)
    return jnp.clip(array, -reach, reach).astype(kind)


def setup_inputs(seed: int = 0, part: int = 0) -> dict:
    splits = jax.random.split(jax.random.key(seed), 10)
    part_keys = jax.random.split(jax.random.fold_in(splits[9], part), 10)
    hidden_in = noise(part_keys[0], (RANKS, ROWS, DS), 1.0, 6.0, ((0, 16),))
    norm_gain = jnp.clip(1.0 + 0.18 * jax.random.normal(splits[1], (D,), jnp.float32), 0.1, 1.9)
    q_blocks = noise(splits[2], (RANKS, QG, HD, D // GC), D ** -0.5, 0.0625, ((0, 16),))
    o_blocks = noise(splits[3], (RANKS, D // GC, QG, HD), (QH * HD // 512) ** -0.5, 1.5, ((0, 16),))
    kv_blocks = noise(splits[4], (2, KVH * HD, D), D ** -0.5, 0.0625, ((2, 16),))
    kv_assign = draw_kv_assign(jax.random.fold_in(splits[9], 71), part)
    key_cache = draw_key_cache(jax.random.fold_in(jax.random.fold_in(splits[9], part), 71), part)
    value_cache = noise(part_keys[7], (RANKS, ROWS, CTXH, HD), 1.0, 6.0, ((0, 16),))
    lengths = draw_lengths(jax.random.fold_in(jax.random.fold_in(splits[9], part), 71), part)
    return dict(hidden_in=hidden_in, norm_gain=norm_gain, q_blocks=q_blocks, o_blocks=o_blocks, kv_blocks=kv_blocks, kv_assign=kv_assign, key_cache=key_cache, value_cache=value_cache, lengths=lengths)


def half_partial(queries, keys, values, valid, key_new, value_new, with_new):
    scale = 1.0 / HD ** 0.5
    scores = jnp.einsum('bmhe,mbte->mbht', queries.astype(jnp.float32), keys.astype(jnp.float32)) * scale
    positions = jnp.arange(CTXH, dtype=jnp.int32)
    masked = positions[None, None, None, :] < valid[:, :, None, None]
    new_score = jnp.einsum('bmhe,bme->mbh', queries.astype(jnp.float32), key_new.astype(jnp.float32)) * scale
    new_score = jnp.where(with_new, new_score, jnp.float32(-1e+30))
    top = jnp.maximum(lax.optimization_barrier(jnp.max(jnp.where(masked, scores, jnp.float32(-1e+30)), axis=-1)), new_score)
    weights = jnp.where(masked, jnp.exp(scores - top[..., None]), jnp.float32(0.0))
    new_weight = jnp.exp(new_score - top)
    total = lax.optimization_barrier(jnp.sum(weights, axis=-1)) + new_weight
    rounded = lax.optimization_barrier(weights.astype(jnp.bfloat16)).astype(jnp.float32)
    new_rounded = lax.optimization_barrier(new_weight.astype(jnp.bfloat16)).astype(jnp.float32)
    summed = jnp.einsum('mbht,mbte->mbhe', rounded, values.astype(jnp.float32))
    summed = summed + new_rounded[..., None] * value_new.astype(jnp.float32).transpose(1, 0, 2)[:, :, None, :]
    return (top, total, summed)

def reference(hidden_in, norm_gain, q_blocks, o_blocks, kv_blocks, kv_assign, key_cache, value_cache, lengths):
    ranks = hidden_in.shape[0]
    groups_count = ranks // ROLL
    grid_cols = ranks // GR
    w_query = q_blocks.reshape(GR, grid_cols, QG, HD, D // grid_cols).transpose(2, 0, 3, 1, 4).reshape(QH * HD, D)
    w_out = o_blocks.reshape(GR, grid_cols, D // grid_cols, QG, HD).transpose(3, 0, 4, 1, 2).reshape(QH * HD, D)
    w_key = kv_blocks[0]
    w_value = kv_blocks[1]
    rows_all = hidden_in.reshape(groups_count, ROLL, ROWS, DS).transpose(0, 2, 1, 3).reshape(groups_count * ROWS, D)
    rows_float = rows_all.astype(jnp.float32)
    mean_square = lax.optimization_barrier(jnp.mean(rows_float * rows_float, axis=-1, keepdims=True))
    normed = (rows_float * lax.rsqrt(mean_square + 1e-05) * norm_gain[None, :]).astype(jnp.bfloat16)
    queries = jnp.dot(normed, w_query.T, preferred_element_type=jnp.float32).astype(jnp.bfloat16)
    key_new = jnp.dot(normed, w_key.T, preferred_element_type=jnp.float32).astype(jnp.bfloat16)
    value_new = jnp.dot(normed, w_value.T, preferred_element_type=jnp.float32).astype(jnp.bfloat16)
    per_group = QH // KVH
    pair_heads = kv_assign[0::2].astype(jnp.int32)
    query_pairs = queries.reshape(groups_count * ROWS, KVH, per_group, HD)[:, pair_heads]
    key_pairs = key_new.reshape(groups_count * ROWS, KVH, HD)[:, pair_heads]
    value_pairs = value_new.reshape(groups_count * ROWS, KVH, HD)[:, pair_heads]
    key_split = key_cache.reshape(groups_count, KVH, 2, ROWS, CTXH, HD)
    value_split = value_cache.reshape(groups_count, KVH, 2, ROWS, CTXH, HD)
    length_split = lengths.reshape(groups_count, KVH, 2, ROWS)

    def one_group(inputs):
        group_queries, group_keys, group_values, group_lengths, group_knew, group_vnew = inputs
        first = half_partial(group_queries, group_keys[:, 0], group_values[:, 0], group_lengths[:, 0], group_knew, group_vnew, True)
        second = half_partial(group_queries, group_keys[:, 1], group_values[:, 1], group_lengths[:, 1], group_knew, group_vnew, False)
        joint = jnp.maximum(first[0], second[0])
        factor_a = jnp.exp(first[0] - joint)
        factor_b = jnp.exp(second[0] - joint)
        numer = first[2] * factor_a[..., None] + second[2] * factor_b[..., None]
        denom = first[1] * factor_a + second[1] * factor_b
        return (numer / denom[..., None]).transpose(1, 0, 2, 3)
    grouped = lax.map(one_group, (query_pairs.reshape(groups_count, ROWS, KVH, per_group, HD), key_split, value_split, length_split, key_pairs.reshape(groups_count, ROWS, KVH, HD), value_pairs.reshape(groups_count, ROWS, KVH, HD)))
    attention = grouped.reshape(groups_count * ROWS, KVH, per_group, HD).astype(jnp.bfloat16)
    head_ids = jnp.arange(KVH, dtype=jnp.int32)
    inverse = lax.optimization_barrier(jnp.sum(head_ids[None, :] * (pair_heads[None, :] == head_ids[:, None]).astype(jnp.int32), axis=1))
    ordered = attention[:, inverse].reshape(groups_count * ROWS, QH * HD)
    result = jnp.dot(ordered, w_out, preferred_element_type=jnp.float32).astype(jnp.bfloat16)
    return result.reshape(groups_count, ROWS, ROLL, DS).transpose(0, 2, 1, 3).reshape(ranks, ROWS, DS)
```

```python
import jax
import jax.numpy as jnp
from jax import lax
from jax.sharding import PartitionSpec as P

D = 8192
KVH = 8
HD = 128
ROLL = 16
ROWS = 8
GR = 4
QG = 16
DS = 512


def from_partner(value, axis, bit):
    mask = 2**bit
    pairs = [(source, source ^ mask) for source in range(lax.axis_size(axis))]
    return lax.ppermute(value, axis, pairs)


def pick(value, ids, axis):
    slices = [
        lax.dynamic_index_in_dim(value, ids[n], axis, keepdims=True) for n in range(ids.shape[0])
    ]
    return jnp.concatenate(slices, axis)


def norm_rows(rows_float, norm_gain):
    mean_square = jnp.mean(rows_float * rows_float, axis=-1, keepdims=True)
    return (rows_float * lax.rsqrt(mean_square + 1e-05) * norm_gain[None, :]).astype(jnp.bfloat16)


def local(
    hidden_in, norm_gain, q_blocks, o_blocks, kv_blocks, kv_assign, key_cache, value_cache, lengths
):
    ranks = lax.axis_size("tp")
    my_index = lax.axis_index("tp")
    my_rank = my_index % ROLL
    my_half = my_rank % 2
    grid_cols = ranks // GR
    group_count = ranks // ROLL
    col_width = q_blocks.shape[3]
    key_width = kv_blocks.shape[2]
    grid_row = my_index // grid_cols
    grid_col = my_index % grid_cols
    dest_rank = jnp.arange(ROLL, dtype=jnp.int32)
    dest_head = kv_assign
    dest_group = 2 * dest_head + dest_rank % 2
    every_rows = lax.all_gather(hidden_in, "tp", axis=0, tiled=True)
    rows_float = (
        every_rows.reshape(group_count, ROLL, ROWS, DS)
        .transpose(0, 2, 1, 3)
        .reshape(group_count * ROWS, D)
        .astype(jnp.float32)
    )
    normed_every = norm_rows(rows_float, norm_gain)
    col_rows = lax.dynamic_slice_in_dim(normed_every, grid_col * col_width, col_width, 1)
    query_part = jnp.einsum(
        "rc,aec->rae", col_rows, q_blocks[0], preferred_element_type=jnp.float32
    )
    query_part = (
        query_part.reshape(group_count, ROWS, QG, HD)
        .transpose(0, 2, 1, 3)
    )
    query_pick = pick(query_part, dest_group, 1).reshape(ranks, ROWS, HD)
    slot_mask = (jnp.arange(GR, dtype=jnp.int32) == grid_row).astype(jnp.float32)
    query_term = (query_pick[:, :, None, :] * slot_mask[None, None, :, None]).reshape(
        ranks, ROWS, GR * HD
    )
    key_rows = lax.dynamic_slice_in_dim(normed_every, my_index * key_width, key_width, 1)
    keyval_part = jnp.einsum("rc,kfc->rkf", key_rows, kv_blocks, preferred_element_type=jnp.float32)
    keyval_part = (
        keyval_part.reshape(group_count, ROWS, 2, KVH, HD)
        .transpose(0, 3, 1, 2, 4)
        .reshape(group_count, KVH, ROWS, 2 * HD)
    )
    keyval_term = pick(keyval_part, dest_head, 1).reshape(ranks, ROWS, 2 * HD)
    proj_term = jnp.concatenate([query_term, keyval_term], -1).reshape(ranks * ROWS, (GR + 2) * HD)
    projected = lax.psum_scatter(proj_term, "tp", scatter_dimension=0, tiled=True)
    queries = projected[:, : GR * HD].astype(jnp.bfloat16)
    keyval_new = projected[:, GR * HD :].astype(jnp.bfloat16)
    key_new = keyval_new[:, :HD]
    value_new = keyval_new[:, HD:]
    partner_queries = from_partner(queries, "tp", 0)
    both_queries = jnp.where(
        my_half == 0,
        jnp.concatenate([queries, partner_queries], 1),
        jnp.concatenate([partner_queries, queries], 1),
    )
    both_queries = both_queries.reshape(ROWS, 2 * GR, HD)
    scale = 1.0 / HD**0.5
    scores = (
        jnp.einsum("bhe,bte->bht", both_queries, key_cache[0], preferred_element_type=jnp.float32)
        * scale
    )
    positions = jnp.arange(scores.shape[2], dtype=jnp.int32)
    masked = positions[None, None, :] < lengths[0][:, None, None]
    new_score = (
        jnp.einsum("bhe,be->bh", both_queries, key_new, preferred_element_type=jnp.float32) * scale
    )
    new_score = jnp.where(my_half == 0, new_score, jnp.float32(-1e30))
    top = jnp.maximum(jnp.max(jnp.where(masked, scores, jnp.float32(-1e30)), axis=-1), new_score)
    weights = jnp.where(masked, jnp.exp(scores - top[..., None]), jnp.float32(0.0))
    new_weight = jnp.exp(new_score - top)
    total = jnp.sum(weights, axis=-1) + new_weight
    summed = jnp.einsum(
        "bht,bte->bhe",
        weights.astype(jnp.bfloat16),
        value_cache[0],
        preferred_element_type=jnp.float32,
    )
    new_rounded = lax.optimization_barrier(new_weight.astype(jnp.bfloat16)).astype(jnp.float32)
    summed = summed + new_rounded[..., None] * value_new.astype(jnp.float32)[:, None, :]
    top_split = top.reshape(ROWS, 2, GR)
    total_split = total.reshape(ROWS, 2, GR)
    summed_split = summed.reshape(ROWS, 2, GR, HD)
    first_half = my_half == 0
    own_top = jnp.where(first_half, top_split[:, 0], top_split[:, 1])
    own_total = jnp.where(first_half, total_split[:, 0], total_split[:, 1])
    own_summed = jnp.where(first_half, summed_split[:, 0], summed_split[:, 1])
    give_top = jnp.where(first_half, top_split[:, 1], top_split[:, 0])
    give_total = jnp.where(first_half, total_split[:, 1], total_split[:, 0])
    give_summed = jnp.where(first_half, summed_split[:, 1], summed_split[:, 0])
    got_top, got_total, got_summed = from_partner((give_top, give_total, give_summed), "tp", 0)
    joint = jnp.maximum(own_top, got_top)
    factor_own = jnp.exp(own_top - joint)
    factor_got = jnp.exp(got_top - joint)
    numer = own_summed * factor_own[..., None] + got_summed * factor_got[..., None]
    denom = own_total * factor_own + got_total * factor_got
    attention = (numer / denom[..., None]).astype(jnp.bfloat16).reshape(ROWS, GR * HD)
    every_attn = lax.all_gather(attention[None], "tp", axis=0, tiled=True)
    head_ids = jnp.arange(KVH, dtype=jnp.int32)
    pair_heads = kv_assign[0::2]
    inverse = jnp.sum(
        head_ids[None, :] * (pair_heads[None, :] == head_ids[:, None]).astype(jnp.int32), axis=1
    )
    slot_ids = jnp.arange(QG, dtype=jnp.int32)
    rank_of_slot = 2 * inverse[slot_ids // 2] + slot_ids % 2
    attn_grid = every_attn.reshape(group_count, ROLL, ROWS, GR, HD)
    row_slot = lax.dynamic_index_in_dim(attn_grid, grid_row, 3, keepdims=False)
    chosen = pick(row_slot, rank_of_slot, 1)
    out_part = jnp.einsum("gabe,cae->gbc", chosen, o_blocks[0], preferred_element_type=jnp.float32)
    placed = jnp.zeros((group_count, ROWS, D), jnp.float32)
    placed = lax.dynamic_update_slice_in_dim(placed, out_part, grid_col * col_width, 2)
    out_term = (
        placed.reshape(group_count, ROWS, ROLL, DS).transpose(0, 2, 1, 3).reshape(ranks * ROWS, DS)
    )
    my_cols = lax.psum_scatter(out_term, "tp", scatter_dimension=0, tiled=True)
    return my_cols.astype(jnp.bfloat16)[None]


def solution(mesh):
    return jax.shard_map(
        local,
        mesh=mesh,
        in_specs=(
            P(("groups", "tp"), None, None),
            P(),
            P("tp", None, None, None),
            P("tp", None, None, None),
            P(None, None, "tp"),
            P(),
            P(("groups", "tp"), None, None, None),
            P(("groups", "tp"), None, None, None),
            P(("groups", "tp"), None),
        ),
        out_specs=P(("groups", "tp"), None, None),
        check_vma=False,
    )
```

```python
import jax
import jax.numpy as jnp
from jax import lax
from jax.experimental import pallas as pl
from jax.experimental.pallas import tpu as pltpu
from jax.sharding import PartitionSpec as P

D = 8192
KVH = 8
HD = 128
ROLL = 16
ROWS = 8
GR = 4
QG = 16
DS = 512


def from_partner(value, axis, bit):
    mask = 2**bit
    pairs = [(source, source ^ mask) for source in range(lax.axis_size(axis))]
    return lax.ppermute(value, axis, pairs)


def pick(value, ids, axis):
    slices = [
        lax.dynamic_index_in_dim(value, ids[n], axis, keepdims=True) for n in range(ids.shape[0])
    ]
    return jnp.concatenate(slices, axis)


def norm_rows(rows_float, norm_gain):
    mean_square = jnp.mean(rows_float * rows_float, axis=-1, keepdims=True)
    return (rows_float * lax.rsqrt(mean_square + 1e-05) * norm_gain[None, :]).astype(jnp.bfloat16)


def local(
    hidden_in, norm_gain, q_blocks, o_blocks, kv_blocks, kv_assign, key_cache, value_cache, lengths
):
    ranks = lax.axis_size("tp")
    my_index = lax.axis_index("tp")
    my_rank = my_index % ROLL
    my_half = my_rank % 2
    grid_cols = ranks // GR
    group_count = ranks // ROLL
    col_width = q_blocks.shape[3]
    key_width = kv_blocks.shape[2]
    grid_row = my_index // grid_cols
    grid_col = my_index % grid_cols
    dest_rank = jnp.arange(ROLL, dtype=jnp.int32)
    dest_head = kv_assign
    dest_group = 2 * dest_head + dest_rank % 2
    every_rows = lax.all_gather(hidden_in, "tp", axis=0, tiled=True)
    rows_float = (
        every_rows.reshape(group_count, ROLL, ROWS, DS)
        .transpose(0, 2, 1, 3)
        .reshape(group_count * ROWS, D)
        .astype(jnp.float32)
    )
    normed_every = norm_rows(rows_float, norm_gain)
    col_rows = lax.dynamic_slice_in_dim(normed_every, grid_col * col_width, col_width, 1)
    query_part = jnp.einsum(
        "rc,aec->rae", col_rows, q_blocks[0], preferred_element_type=jnp.float32
    )
    query_part = (
        query_part.reshape(group_count, ROWS, QG, HD)
        .transpose(0, 2, 1, 3)
    )
    query_pick = pick(query_part, dest_group, 1).reshape(ranks, ROWS, HD)
    slot_mask = (jnp.arange(GR, dtype=jnp.int32) == grid_row).astype(jnp.float32)
    query_term = (query_pick[:, :, None, :] * slot_mask[None, None, :, None]).reshape(
        ranks, ROWS, GR * HD
    )
    key_rows = lax.dynamic_slice_in_dim(normed_every, my_index * key_width, key_width, 1)
    keyval_part = jnp.einsum("rc,kfc->rkf", key_rows, kv_blocks, preferred_element_type=jnp.float32)
    keyval_part = (
        keyval_part.reshape(group_count, ROWS, 2, KVH, HD)
        .transpose(0, 3, 1, 2, 4)
        .reshape(group_count, KVH, ROWS, 2 * HD)
    )
    keyval_term = pick(keyval_part, dest_head, 1).reshape(ranks, ROWS, 2 * HD)
    proj_term = jnp.concatenate([query_term, keyval_term], -1).reshape(ranks * ROWS, (GR + 2) * HD)
    projected = lax.psum_scatter(proj_term, "tp", scatter_dimension=0, tiled=True)
    queries = projected[:, : GR * HD].astype(jnp.bfloat16)
    keyval_new = projected[:, GR * HD :].astype(jnp.bfloat16)
    key_new = keyval_new[:, :HD]
    value_new = keyval_new[:, HD:]
    partner_queries = from_partner(queries, "tp", 0)
    both_queries = jnp.where(
        my_half == 0,
        jnp.concatenate([queries, partner_queries], 1),
        jnp.concatenate([partner_queries, queries], 1),
    )
    both_queries = both_queries.reshape(ROWS, 2 * GR, HD)
    scale = 1.0 / HD**0.5
    scores = (
        jnp.einsum("bhe,bte->bht", both_queries, key_cache[0], preferred_element_type=jnp.float32)
        * scale
    )
    positions = jnp.arange(scores.shape[2], dtype=jnp.int32)
    masked = positions[None, None, :] < lengths[0][:, None, None]
    new_score = (
        jnp.einsum("bhe,be->bh", both_queries, key_new, preferred_element_type=jnp.float32) * scale
    )
    new_score = jnp.where(my_half == 0, new_score, jnp.float32(-1e30))
    top = jnp.maximum(jnp.max(jnp.where(masked, scores, jnp.float32(-1e30)), axis=-1), new_score)
    weights = jnp.where(masked, jnp.exp(scores - top[..., None]), jnp.float32(0.0))
    new_weight = jnp.exp(new_score - top)
    total = jnp.sum(weights, axis=-1) + new_weight
    summed = jnp.einsum(
        "bht,bte->bhe",
        weights.astype(jnp.bfloat16),
        value_cache[0],
        preferred_element_type=jnp.float32,
    )
    new_rounded = lax.optimization_barrier(new_weight.astype(jnp.bfloat16)).astype(jnp.float32)
    summed = summed + new_rounded[..., None] * value_new.astype(jnp.float32)[:, None, :]
    top_split = top.reshape(ROWS, 2, GR)
    total_split = total.reshape(ROWS, 2, GR)
    summed_split = summed.reshape(ROWS, 2, GR, HD)
    first_half = my_half == 0
    own_top = jnp.where(first_half, top_split[:, 0], top_split[:, 1])
    own_total = jnp.where(first_half, total_split[:, 0], total_split[:, 1])
    own_summed = jnp.where(first_half, summed_split[:, 0], summed_split[:, 1])
    give_top = jnp.where(first_half, top_split[:, 1], top_split[:, 0])
    give_total = jnp.where(first_half, total_split[:, 1], total_split[:, 0])
    give_summed = jnp.where(first_half, summed_split[:, 1], summed_split[:, 0])
    got_top, got_total, got_summed = from_partner((give_top, give_total, give_summed), "tp", 0)
    joint = jnp.maximum(own_top, got_top)
    factor_own = jnp.exp(own_top - joint)
    factor_got = jnp.exp(got_top - joint)
    numer = own_summed * factor_own[..., None] + got_summed * factor_got[..., None]
    denom = own_total * factor_own + got_total * factor_got
    attention = (numer / denom[..., None]).astype(jnp.bfloat16).reshape(ROWS, GR * HD)
    every_attn = lax.all_gather(attention[None], "tp", axis=0, tiled=True)
    head_ids = jnp.arange(KVH, dtype=jnp.int32)
    pair_heads = kv_assign[0::2]
    inverse = jnp.sum(
        head_ids[None, :] * (pair_heads[None, :] == head_ids[:, None]).astype(jnp.int32), axis=1
    )
    slot_ids = jnp.arange(QG, dtype=jnp.int32)
    rank_of_slot = 2 * inverse[slot_ids // 2] + slot_ids % 2
    attn_grid = every_attn.reshape(group_count, ROLL, ROWS, GR, HD)
    row_slot = lax.dynamic_index_in_dim(attn_grid, grid_row, 3, keepdims=False)
    chosen = pick(row_slot, rank_of_slot, 1)
    out_part = jnp.einsum("gabe,cae->gbc", chosen, o_blocks[0], preferred_element_type=jnp.float32)
    placed = jnp.zeros((group_count, ROWS, D), jnp.float32)
    placed = lax.dynamic_update_slice_in_dim(placed, out_part, grid_col * col_width, 2)
    out_term = (
        placed.reshape(group_count, ROWS, ROLL, DS).transpose(0, 2, 1, 3).reshape(ranks * ROWS, DS)
    )
    my_cols = lax.psum_scatter(out_term, "tp", scatter_dimension=0, tiled=True)
    return my_cols.astype(jnp.bfloat16)[None]


def pair_kernel(
    hidden_ref, gain_ref, assign_ref, lengths_ref, q_hbm, o_hbm, kv_hbm, key_hbm, value_hbm,
    out_ref,
    q_ref, o_ref, ot_ref, kv_ref, key_ref, value_ref,
    x_send, x_recv, sq_send, sq_recv, qpart, kvpart, q_send, q_recv, kv_send, kv_recv,
    queries, stats, stats_recv, at_send, at_recv, normed, ordered, part_send, part_recv,
    load_sem, qload_sem, x_ssem, x_rsem, sq_ssem, sq_rsem, q_ssem, q_rsem, kv_ssem, kv_rsem,
    st_ssem, st_rsem, at_ssem, at_rsem, part_ssem, part_rsem,
):
    me = lax.axis_index("tp")
    row = me // GR
    col = me % GR
    half = me % 2
    bf16 = jnp.bfloat16
    f32 = jnp.float32

    def remote(src, dst, send, recv, dest):
        return pltpu.make_async_remote_copy(
            src_ref=src, dst_ref=dst, send_sem=send, recv_sem=recv,
            device_id={"tp": dest}, device_id_type=pl.DeviceIdType.MESH,
        )

    def peers(body):
        def step(p, carry):
            body(lax.rem(me + p, ROLL))
            return carry
        lax.fori_loop(1, ROLL, step, 0)

    barrier = pltpu.get_barrier_semaphore()
    peers(lambda peer: pl.semaphore_signal(
        barrier, inc=1, device_id={"tp": peer}, device_id_type=pl.DeviceIdType.MESH))

    kv_load = pltpu.make_async_copy(kv_hbm, kv_ref, load_sem.at[0])
    kv_load.start()
    q_loads = []
    for n in range(KVH):
        span = pl.ds(n * 256, 256)
        q_loads.append(pltpu.make_async_copy(q_hbm.at[span], q_ref.at[span], qload_sem.at[n]))
        q_loads[n].start()

    own = hidden_ref[0].astype(f32)
    packed = jnp.concatenate([own[:, :256], own[:, 256:]], 0).astype(bf16)
    x_send[...] = packed
    squares = jnp.sum(own * own, axis=-1, keepdims=True)
    diagonal = lax.broadcasted_iota(jnp.int32, (ROWS, 128), 0) == lax.broadcasted_iota(
        jnp.int32, (ROWS, 128), 1)
    sq_row = jnp.sum(jnp.where(diagonal, squares, 0.0), axis=0, keepdims=True)
    sq_send[0] = sq_row
    sq_recv[me] = sq_row

    @pl.when(row == col)
    def _():
        x_recv[col] = packed

    @pl.when(half == 1)
    def _():
        kv_recv[...] = jnp.zeros_like(kv_recv)

    pl.semaphore_wait(barrier, ROLL - 1)
    peers(lambda peer: remote(
        sq_send.at[0], sq_recv.at[me], sq_ssem.at[peer], sq_rsem.at[me], peer).start())

    def x_copy(i):
        return remote(x_send, x_recv.at[col], x_ssem.at[i], x_rsem.at[col], GR * i + row)

    for i in range(GR):
        pl.when(GR * i + row != me)(lambda i=i: x_copy(i).start())

    o_load = pltpu.make_async_copy(o_hbm, o_ref, load_sem.at[1])
    key_load = pltpu.make_async_copy(key_hbm, key_ref, load_sem.at[2])
    value_load = pltpu.make_async_copy(value_hbm, value_ref, load_sem.at[3])
    o_load.start()
    key_load.start()
    value_load.start()

    peers(lambda peer: remote(
        sq_send.at[0], sq_recv.at[peer], sq_ssem.at[peer], sq_rsem.at[peer], peer).wait_recv())
    total_sq = jnp.sum(sq_recv[...], axis=0)
    mean_sq = jnp.sum(jnp.where(diagonal, total_sq, 0.0), axis=-1, keepdims=True) * (1.0 / D)
    inv_root = lax.rsqrt(mean_sq + 1e-05)

    own_normed = jnp.concatenate([
        own[:, t * 128:(t + 1) * 128] * inv_root * gain_ref[pl.ds(me * 4 + t, 1), :]
        for t in range(4)], 1).astype(bf16)
    kv_load.wait()
    contract = (((1,), (1,)), ((), ()))
    for c in range(2):
        made = lax.dot_general(own_normed, kv_ref[c], contract, preferred_element_type=f32)
        for g in range(KVH):
            kvpart[g, :, c * HD:(c + 1) * HD] = made[:, g * HD:(g + 1) * HD]

    def kv_copy(m):
        return remote(
            kv_send.at[m], kv_recv.at[me], kv_ssem.at[m], kv_rsem.at[me], 2 * m)

    def kv_step(m, carry):
        term = kvpart[assign_ref[2 * m]]
        kv_send[m] = term

        @pl.when(2 * m == me)
        def _():
            kv_recv[me] = term

        pl.when(2 * m != me)(lambda: kv_copy(m).start())
        return carry
    lax.fori_loop(0, KVH, kv_step, 0)

    for k in range(GR):
        pl.when(GR * col + k != me)(lambda k=k: remote(
            x_send, x_recv.at[k], x_ssem.at[k], x_rsem.at[k], GR * col + k).wait_recv())
        block = x_recv[k].astype(f32)
        for t in range(4):
            lo = (t % 2) * 128
            tile = block[(t // 2) * ROWS:(t // 2 + 1) * ROWS, lo:lo + 128]
            gain = gain_ref[pl.ds(16 * col + 4 * k + t, 1), :]
            at = k * 512 + t * 128
            normed[:, at:at + 128] = (tile * inv_root * gain).astype(bf16)
    for n in range(KVH):
        q_loads[n].wait()
        qpart[n] = lax.dot_general(
            normed[...], q_ref[n * 256:(n + 1) * 256, :], contract, preferred_element_type=f32)

    q_own = qpart[assign_ref[me]]
    q_recv[me] = q_own

    def q_start(peer):
        q_send[peer] = qpart[assign_ref[peer]]
        remote(q_send.at[peer], q_recv.at[me], q_ssem.at[peer], q_rsem.at[me], peer).start()
    peers(q_start)

    o_load.wait()
    r_ids = lax.broadcasted_iota(jnp.int32, (256, 256), 0)
    c_ids = lax.broadcasted_iota(jnp.int32, (256, 256), 1)
    shuffle = jnp.where(c_ids == (r_ids % 16) * 16 + r_ids // 16, 1.0, 0.0).astype(bf16)

    def turn(n, carry):
        base = pl.multiple_of(n * 512, 512)
        rhs = jnp.concatenate(
            [o_ref[pl.ds(base, 256), :], o_ref[pl.ds(base + 256, 256), :]], 1)
        turned = jnp.dot(shuffle, rhs, preferred_element_type=f32).astype(bf16)
        to = pl.multiple_of(n * 32, 32)
        for a in range(QG):
            for u in range(2):
                ot_ref[pl.ds(to + 16 * u, 16), a * HD:(a + 1) * HD] = turned[
                    a * 16:(a + 1) * 16, u * 128:(u + 1) * 128]
        return carry
    lax.fori_loop(0, 64, turn, 0)

    @pl.when(half == 0)
    def _():
        peers(lambda peer: remote(
            kv_send.at[0], kv_recv.at[peer], kv_ssem.at[0], kv_rsem.at[peer], peer).wait_recv())
    peers(lambda peer: remote(
        q_send.at[peer], q_recv.at[peer], q_ssem.at[peer], q_rsem.at[peer], peer).wait_recv())
    for i in range(GR):
        q_sum = (q_recv[4 * i] + q_recv[4 * i + 1]) + (q_recv[4 * i + 2] + q_recv[4 * i + 3])
        for s in range(2):
            queries[:, s * GR + i, :] = q_sum[:, s * HD:(s + 1) * HD]
    kv_new = jnp.sum(kv_recv[...], axis=0).astype(bf16).astype(f32)
    key_load.wait()
    value_load.wait()
    scale = 1.0 / HD**0.5
    positions = lax.broadcasted_iota(jnp.int32, (8, key_ref.shape[1]), 1)
    for b in range(ROWS):
        q_b = queries[b].astype(bf16)
        scores = lax.dot_general(q_b, key_ref[b], contract, preferred_element_type=f32) * scale
        masked = positions < lengths_ref[0, b]
        scores = jnp.where(masked, scores, -1e30)
        new_score = jnp.sum(
            q_b.astype(f32) * kv_new[b:b + 1, :HD], axis=-1, keepdims=True) * scale
        new_score = jnp.where(half == 0, new_score, -1e30)
        top = jnp.maximum(jnp.max(scores, axis=-1, keepdims=True), new_score)
        weights = jnp.where(masked, jnp.exp(scores - top), 0.0)
        new_weight = jnp.exp(new_score - top)
        total = jnp.sum(weights, axis=-1, keepdims=True) + new_weight
        summed = jnp.dot(weights.astype(bf16), value_ref[b], preferred_element_type=f32)
        summed = summed + new_weight.astype(bf16).astype(f32) * kv_new[b:b + 1, HD:]
        stats[b, 0] = summed
        stats[b, 1] = jnp.broadcast_to(top, (8, HD))
        stats[b, 2] = jnp.broadcast_to(total, (8, HD))

    st_copy = remote(
        stats.at[pl.ds(4 * (1 - half), 4)], stats_recv, st_ssem, st_rsem, me + 1 - 2 * half)
    st_copy.start()
    st_copy.wait_recv()
    for b in range(4):
        mine = stats[4 * half + b]
        got = stats_recv[b]
        joint = jnp.maximum(mine[1], got[1])
        f_mine = jnp.exp(mine[1] - joint)
        f_got = jnp.exp(got[1] - joint)
        merged = (mine[0] * f_mine + got[0] * f_got) / (mine[2] * f_mine + got[2] * f_got)
        for s in range(2):
            at_send[:, s * 4 + b, :] = merged[s * 4:(s + 1) * 4]

    at_recv[me] = at_send[row]
    peers(lambda peer: remote(
        at_send.at[peer // GR], at_recv.at[me], at_ssem.at[peer], at_rsem.at[me], peer).start())
    peers(lambda peer: remote(
        at_send.at[0], at_recv.at[peer], at_ssem.at[peer], at_rsem.at[peer], peer).wait_recv())

    for g in range(KVH):
        place = jnp.int32(0)
        for m in range(1, KVH):
            place = jnp.where(assign_ref[2 * m] == g, m, place)
        first = at_recv[2 * place]
        second = at_recv[2 * place + 1]
        for s in range(2):
            a = 2 * g + s
            ordered[:, a * HD:(a + 1) * HD] = jnp.concatenate(
                [first[s * 4:(s + 1) * 4], second[s * 4:(s + 1) * 4]], 0).astype(bf16)

    def part_copy(k):
        return remote(
            part_send.at[k], part_recv.at[row], part_ssem.at[k], part_rsem.at[row], GR * col + k)

    for k in range(GR):
        part = lax.dot_general(
            ordered[...], ot_ref[k * 512:(k + 1) * 512, :], contract, preferred_element_type=f32)
        part_send[k] = part

        @pl.when(GR * col + k == me)
        def _(part=part):
            part_recv[row] = part

        pl.when(GR * col + k != me)(lambda k=k: part_copy(k).start())
    for i in range(GR):
        pl.when(GR * i + row != me)(lambda i=i: remote(
            part_send.at[0], part_recv.at[i], part_ssem.at[0], part_rsem.at[i],
            GR * i + row).wait_recv())
    out_ref[0] = (
        (part_recv[0] + part_recv[1]) + (part_recv[2] + part_recv[3])).astype(bf16)

    def drain(peer):
        remote(sq_send.at[0], sq_recv.at[me], sq_ssem.at[peer], sq_rsem.at[me], peer).wait_send()
        remote(q_send.at[peer], q_recv.at[me], q_ssem.at[peer], q_rsem.at[me], peer).wait_send()
        remote(at_send.at[0], at_recv.at[me], at_ssem.at[peer], at_rsem.at[me], peer).wait_send()
    peers(drain)
    for m in range(KVH):
        pl.when(2 * m != me)(lambda m=m: kv_copy(m).wait_send())
    for i in range(GR):
        pl.when(GR * i + row != me)(lambda i=i: x_copy(i).wait_send())
        pl.when(GR * col + i != me)(lambda i=i: part_copy(i).wait_send())
    st_copy.wait_send()


def one_group(
    hidden_in, norm_gain, q_blocks, o_blocks, kv_blocks, kv_assign, key_cache, value_cache, lengths
):
    f32, bf16 = jnp.float32, jnp.bfloat16
    ctx = key_cache.shape[2]
    vmem = pl.BlockSpec(memory_space=pltpu.VMEM)
    smem = pl.BlockSpec(memory_space=pltpu.SMEM)
    hbm = pl.BlockSpec(memory_space=pl.ANY)
    dma = pltpu.SemaphoreType.DMA
    return pl.pallas_call(
        pair_kernel,
        out_shape=jax.ShapeDtypeStruct((1, ROWS, DS), bf16),
        in_specs=[vmem, vmem, smem, smem, hbm, hbm, hbm, hbm, hbm],
        out_specs=vmem,
        scratch_shapes=[
            pltpu.VMEM((2048, 2048), bf16),
            pltpu.VMEM((32768, 128), bf16),
            pltpu.VMEM((2048, 2048), bf16),
            pltpu.VMEM((2, 1024, DS), bf16),
            pltpu.VMEM((ROWS, ctx, HD), bf16),
            pltpu.VMEM((ROWS, ctx, HD), bf16),
            pltpu.VMEM((16, 256), bf16),
            pltpu.VMEM((GR, 16, 256), bf16),
            pltpu.VMEM((1, 1, 128), f32),
            pltpu.VMEM((ROLL, 1, 128), f32),
            pltpu.VMEM((KVH, ROWS, 256), f32),
            pltpu.VMEM((KVH, ROWS, 256), f32),
            pltpu.VMEM((ROLL, ROWS, 256), f32),
            pltpu.VMEM((ROLL, ROWS, 256), f32),
            pltpu.VMEM((KVH, ROWS, 256), f32),
            pltpu.VMEM((ROLL, ROWS, 256), f32),
            pltpu.VMEM((ROWS, 8, HD), f32),
            pltpu.VMEM((ROWS, 3, 8, HD), f32),
            pltpu.VMEM((4, 3, 8, HD), f32),
            pltpu.VMEM((GR, 8, HD), f32),
            pltpu.VMEM((ROLL, 8, HD), f32),
            pltpu.VMEM((ROWS, 2048), bf16),
            pltpu.VMEM((ROWS, 2048), bf16),
            pltpu.VMEM((GR, ROWS, DS), f32),
            pltpu.VMEM((GR, ROWS, DS), f32),
            dma((4,)), dma((KVH,)),
            dma((GR,)), dma((GR,)),
            dma((ROLL,)), dma((ROLL,)),
            dma((ROLL,)), dma((ROLL,)),
            dma((KVH,)), dma((ROLL,)),
            dma, dma,
            dma((ROLL,)), dma((ROLL,)),
            dma((GR,)), dma((GR,)),
        ],
        compiler_params=pltpu.CompilerParams(
            collective_id=0, has_side_effects=True, vmem_limit_bytes=56 * 2**20),
        cost_estimate=pl.CostEstimate(
            flops=2 * 8 * 11 * 2**20, bytes_accessed=26 * 2**20, transcendentals=8 * 8 * ctx),
    )(
        hidden_in, norm_gain.reshape(-1, 128), kv_assign, lengths,
        q_blocks.reshape(2048, 2048), o_blocks.reshape(-1, HD), kv_blocks,
        key_cache[0], value_cache[0],
    )


def solution(mesh):
    return jax.shard_map(
        one_group if mesh.shape["tp"] == ROLL else local,
        mesh=mesh,
        in_specs=(
            P(("groups", "tp"), None, None),
            P(),
            P("tp", None, None, None),
            P("tp", None, None, None),
            P(None, None, "tp"),
            P(),
            P(("groups", "tp"), None, None, None),
            P(("groups", "tp"), None, None, None),
            P(("groups", "tp"), None),
        ),
        out_specs=P(("groups", "tp"), None, None),
        check_vma=False,
    )
```

```python
import jax
import jax.numpy as jnp
from jax import lax
from jax.experimental import pallas as pl
from jax.experimental.pallas import tpu as pltpu
from jax.sharding import PartitionSpec as P

D = 8192
KVH = 8
HD = 128
ROLL = 16
ROWS = 8
GR = 4
QG = 16
DS = 512


def from_partner(value, axis, bit):
    mask = 2**bit
    pairs = [(source, source ^ mask) for source in range(lax.axis_size(axis))]
    return lax.ppermute(value, axis, pairs)


def pick(value, ids, axis):
    slices = [
        lax.dynamic_index_in_dim(value, ids[n], axis, keepdims=True) for n in range(ids.shape[0])
    ]
    return jnp.concatenate(slices, axis)


def norm_rows(rows_float, norm_gain):
    mean_square = jnp.mean(rows_float * rows_float, axis=-1, keepdims=True)
    return (rows_float * lax.rsqrt(mean_square + 1e-05) * norm_gain[None, :]).astype(jnp.bfloat16)


def local(
    hidden_in, norm_gain, q_blocks, o_blocks, kv_blocks, kv_assign, key_cache, value_cache, lengths
):
    ranks = lax.axis_size("tp")
    my_index = lax.axis_index("tp")
    my_rank = my_index % ROLL
    my_half = my_rank % 2
    grid_cols = ranks // GR
    group_count = ranks // ROLL
    col_width = q_blocks.shape[3]
    key_width = kv_blocks.shape[2]
    grid_row = my_index // grid_cols
    grid_col = my_index % grid_cols
    dest_rank = jnp.arange(ROLL, dtype=jnp.int32)
    dest_head = kv_assign
    dest_group = 2 * dest_head + dest_rank % 2
    every_rows = lax.all_gather(hidden_in, "tp", axis=0, tiled=True)
    rows_float = (
        every_rows.reshape(group_count, ROLL, ROWS, DS)
        .transpose(0, 2, 1, 3)
        .reshape(group_count * ROWS, D)
        .astype(jnp.float32)
    )
    normed_every = norm_rows(rows_float, norm_gain)
    col_rows = lax.dynamic_slice_in_dim(normed_every, grid_col * col_width, col_width, 1)
    query_part = jnp.einsum(
        "rc,aec->rae", col_rows, q_blocks[0], preferred_element_type=jnp.float32
    )
    query_part = (
        query_part.reshape(group_count, ROWS, QG, HD)
        .transpose(0, 2, 1, 3)
    )
    query_pick = pick(query_part, dest_group, 1).reshape(ranks, ROWS, HD)
    slot_mask = (jnp.arange(GR, dtype=jnp.int32) == grid_row).astype(jnp.float32)
    query_term = (query_pick[:, :, None, :] * slot_mask[None, None, :, None]).reshape(
        ranks, ROWS, GR * HD
    )
    key_rows = lax.dynamic_slice_in_dim(normed_every, my_index * key_width, key_width, 1)
    keyval_part = jnp.einsum("rc,kfc->rkf", key_rows, kv_blocks, preferred_element_type=jnp.float32)
    keyval_part = (
        keyval_part.reshape(group_count, ROWS, 2, KVH, HD)
        .transpose(0, 3, 1, 2, 4)
        .reshape(group_count, KVH, ROWS, 2 * HD)
    )
    keyval_term = pick(keyval_part, dest_head, 1).reshape(ranks, ROWS, 2 * HD)
    proj_term = jnp.concatenate([query_term, keyval_term], -1).reshape(ranks * ROWS, (GR + 2) * HD)
    projected = lax.psum_scatter(proj_term, "tp", scatter_dimension=0, tiled=True)
    queries = projected[:, : GR * HD].astype(jnp.bfloat16)
    keyval_new = projected[:, GR * HD :].astype(jnp.bfloat16)
    key_new = keyval_new[:, :HD]
    value_new = keyval_new[:, HD:]
    partner_queries = from_partner(queries, "tp", 0)
    both_queries = jnp.where(
        my_half == 0,
        jnp.concatenate([queries, partner_queries], 1),
        jnp.concatenate([partner_queries, queries], 1),
    )
    both_queries = both_queries.reshape(ROWS, 2 * GR, HD)
    scale = 1.0 / HD**0.5
    scores = (
        jnp.einsum("bhe,bte->bht", both_queries, key_cache[0], preferred_element_type=jnp.float32)
        * scale
    )
    positions = jnp.arange(scores.shape[2], dtype=jnp.int32)
    masked = positions[None, None, :] < lengths[0][:, None, None]
    new_score = (
        jnp.einsum("bhe,be->bh", both_queries, key_new, preferred_element_type=jnp.float32) * scale
    )
    new_score = jnp.where(my_half == 0, new_score, jnp.float32(-1e30))
    top = jnp.maximum(jnp.max(jnp.where(masked, scores, jnp.float32(-1e30)), axis=-1), new_score)
    weights = jnp.where(masked, jnp.exp(scores - top[..., None]), jnp.float32(0.0))
    new_weight = jnp.exp(new_score - top)
    total = jnp.sum(weights, axis=-1) + new_weight
    summed = jnp.einsum(
        "bht,bte->bhe",
        weights.astype(jnp.bfloat16),
        value_cache[0],
        preferred_element_type=jnp.float32,
    )
    new_rounded = lax.optimization_barrier(new_weight.astype(jnp.bfloat16)).astype(jnp.float32)
    summed = summed + new_rounded[..., None] * value_new.astype(jnp.float32)[:, None, :]
    top_split = top.reshape(ROWS, 2, GR)
    total_split = total.reshape(ROWS, 2, GR)
    summed_split = summed.reshape(ROWS, 2, GR, HD)
    first_half = my_half == 0
    own_top = jnp.where(first_half, top_split[:, 0], top_split[:, 1])
    own_total = jnp.where(first_half, total_split[:, 0], total_split[:, 1])
    own_summed = jnp.where(first_half, summed_split[:, 0], summed_split[:, 1])
    give_top = jnp.where(first_half, top_split[:, 1], top_split[:, 0])
    give_total = jnp.where(first_half, total_split[:, 1], total_split[:, 0])
    give_summed = jnp.where(first_half, summed_split[:, 1], summed_split[:, 0])
    got_top, got_total, got_summed = from_partner((give_top, give_total, give_summed), "tp", 0)
    joint = jnp.maximum(own_top, got_top)
    factor_own = jnp.exp(own_top - joint)
    factor_got = jnp.exp(got_top - joint)
    numer = own_summed * factor_own[..., None] + got_summed * factor_got[..., None]
    denom = own_total * factor_own + got_total * factor_got
    attention = (numer / denom[..., None]).astype(jnp.bfloat16).reshape(ROWS, GR * HD)
    every_attn = lax.all_gather(attention[None], "tp", axis=0, tiled=True)
    head_ids = jnp.arange(KVH, dtype=jnp.int32)
    pair_heads = kv_assign[0::2]
    inverse = jnp.sum(
        head_ids[None, :] * (pair_heads[None, :] == head_ids[:, None]).astype(jnp.int32), axis=1
    )
    slot_ids = jnp.arange(QG, dtype=jnp.int32)
    rank_of_slot = 2 * inverse[slot_ids // 2] + slot_ids % 2
    attn_grid = every_attn.reshape(group_count, ROLL, ROWS, GR, HD)
    row_slot = lax.dynamic_index_in_dim(attn_grid, grid_row, 3, keepdims=False)
    chosen = pick(row_slot, rank_of_slot, 1)
    out_part = jnp.einsum("gabe,cae->gbc", chosen, o_blocks[0], preferred_element_type=jnp.float32)
    placed = jnp.zeros((group_count, ROWS, D), jnp.float32)
    placed = lax.dynamic_update_slice_in_dim(placed, out_part, grid_col * col_width, 2)
    out_term = (
        placed.reshape(group_count, ROWS, ROLL, DS).transpose(0, 2, 1, 3).reshape(ranks * ROWS, DS)
    )
    my_cols = lax.psum_scatter(out_term, "tp", scatter_dimension=0, tiled=True)
    return my_cols.astype(jnp.bfloat16)[None]


def pair_kernel(
    hidden_ref, gain_ref, assign_ref, lengths_ref, q_hbm, o_hbm, kv_hbm, key_hbm, value_hbm,
    out_ref,
    q_ref, o_ref, ot_ref, kv_ref, key_ref, value_ref,
    x_send, x_recv, sq_send, sq_recv, qpart, kvpart, q_send, q_recv, kv_send, kv_recv,
    queries, stats, stats_recv, at_send, at_recv, normed, ordered, part_send, part_recv,
    load_sem, qload_sem, x_ssem, x_rsem, sq_ssem, sq_rsem, q_ssem, q_rsem, kv_ssem, kv_rsem,
    st_ssem, st_rsem, at_ssem, at_rsem, part_ssem, part_rsem,
):
    me = lax.axis_index("tp")
    row = me // GR
    col = me % GR
    half = me % 2
    bf16 = jnp.bfloat16
    f32 = jnp.float32

    def remote(src, dst, send, recv, dest):
        return pltpu.make_async_remote_copy(
            src_ref=src, dst_ref=dst, send_sem=send, recv_sem=recv,
            device_id={"tp": dest}, device_id_type=pl.DeviceIdType.MESH,
        )

    def peers(body):
        def step(p, carry):
            body(lax.rem(me + p, ROLL))
            return carry
        lax.fori_loop(1, ROLL, step, 0)

    barrier = pltpu.get_barrier_semaphore()
    peers(lambda peer: pl.semaphore_signal(
        barrier, inc=1, device_id={"tp": peer}, device_id_type=pl.DeviceIdType.MESH))

    kv_load = pltpu.make_async_copy(kv_hbm, kv_ref, load_sem.at[0])
    kv_load.start()
    q_loads = []
    for n in range(KVH):
        span = pl.ds(n * 256, 256)
        q_loads.append(pltpu.make_async_copy(q_hbm.at[span], q_ref.at[span], qload_sem.at[n]))
        q_loads[n].start()

    own = hidden_ref[0].astype(f32)
    packed = jnp.concatenate([own[:, :256], own[:, 256:]], 0).astype(bf16)
    x_send[...] = packed
    squares = jnp.sum(own * own, axis=-1, keepdims=True)
    diagonal = lax.broadcasted_iota(jnp.int32, (ROWS, 128), 0) == lax.broadcasted_iota(
        jnp.int32, (ROWS, 128), 1)
    sq_row = jnp.sum(jnp.where(diagonal, squares, 0.0), axis=0, keepdims=True)
    sq_send[0] = sq_row
    sq_recv[me] = sq_row

    @pl.when(row == col)
    def _():
        x_recv[col] = packed

    @pl.when(half == 1)
    def _():
        kv_recv[...] = jnp.zeros_like(kv_recv)

    pl.semaphore_wait(barrier, ROLL - 1)
    peers(lambda peer: remote(
        sq_send.at[0], sq_recv.at[me], sq_ssem.at[peer], sq_rsem.at[me], peer).start())

    def x_copy(i):
        return remote(x_send, x_recv.at[col], x_ssem.at[i], x_rsem.at[col], GR * i + row)

    for i in range(GR):
        pl.when(GR * i + row != me)(lambda i=i: x_copy(i).start())

    o_load = pltpu.make_async_copy(o_hbm, o_ref, load_sem.at[1])
    key_load = pltpu.make_async_copy(key_hbm, key_ref, load_sem.at[2])
    value_load = pltpu.make_async_copy(value_hbm, value_ref, load_sem.at[3])
    o_load.start()
    key_load.start()
    value_load.start()

    peers(lambda peer: remote(
        sq_send.at[0], sq_recv.at[peer], sq_ssem.at[peer], sq_rsem.at[peer], peer).wait_recv())
    total_sq = jnp.sum(sq_recv[...], axis=0)
    mean_sq = jnp.sum(jnp.where(diagonal, total_sq, 0.0), axis=-1, keepdims=True) * (1.0 / D)
    inv_root = lax.rsqrt(mean_sq + 1e-05)

    own_normed = jnp.concatenate([
        own[:, t * 128:(t + 1) * 128] * inv_root * gain_ref[pl.ds(me * 4 + t, 1), :]
        for t in range(4)], 1).astype(bf16)
    kv_load.wait()
    contract = (((1,), (1,)), ((), ()))
    for c in range(2):
        made = lax.dot_general(own_normed, kv_ref[c], contract, preferred_element_type=f32)
        for g in range(KVH):
            kvpart[g, :, c * HD:(c + 1) * HD] = made[:, g * HD:(g + 1) * HD]

    def kv_copy(m):
        return remote(
            kv_send.at[m], kv_recv.at[me], kv_ssem.at[m], kv_rsem.at[me], 2 * m)

    def kv_step(m, carry):
        term = kvpart[assign_ref[2 * m]]
        kv_send[m] = term

        @pl.when(2 * m == me)
        def _():
            kv_recv[me] = term

        pl.when(2 * m != me)(lambda: kv_copy(m).start())
        return carry
    lax.fori_loop(0, KVH, kv_step, 0)

    for k in range(GR):
        pl.when(GR * col + k != me)(lambda k=k: remote(
            x_send, x_recv.at[k], x_ssem.at[k], x_rsem.at[k], GR * col + k).wait_recv())
        block = x_recv[k].astype(f32)
        for t in range(4):
            lo = (t % 2) * 128
            tile = block[(t // 2) * ROWS:(t // 2 + 1) * ROWS, lo:lo + 128]
            gain = gain_ref[pl.ds(16 * col + 4 * k + t, 1), :]
            at = k * 512 + t * 128
            normed[:, at:at + 128] = (tile * inv_root * gain).astype(bf16)
    for n in range(KVH):
        q_loads[n].wait()
        qpart[n] = lax.dot_general(
            normed[...], q_ref[n * 256:(n + 1) * 256, :], contract, preferred_element_type=f32)

    q_own = qpart[assign_ref[me]]
    q_recv[me] = q_own

    def q_start(peer):
        q_send[peer] = qpart[assign_ref[peer]]
        remote(q_send.at[peer], q_recv.at[me], q_ssem.at[peer], q_rsem.at[me], peer).start()
    peers(q_start)

    o_load.wait()
    r_ids = lax.broadcasted_iota(jnp.int32, (256, 256), 0)
    c_ids = lax.broadcasted_iota(jnp.int32, (256, 256), 1)
    shuffle = jnp.where(c_ids == (r_ids % 16) * 16 + r_ids // 16, 1.0, 0.0).astype(bf16)

    def turn(n, carry):
        base = pl.multiple_of(n * 512, 512)
        rhs = jnp.concatenate(
            [o_ref[pl.ds(base, 256), :], o_ref[pl.ds(base + 256, 256), :]], 1)
        turned = jnp.dot(shuffle, rhs, preferred_element_type=f32).astype(bf16)
        to = pl.multiple_of(n * 32, 32)
        for a in range(QG):
            for u in range(2):
                ot_ref[pl.ds(to + 16 * u, 16), a * HD:(a + 1) * HD] = turned[
                    a * 16:(a + 1) * 16, u * 128:(u + 1) * 128]
        return carry

    def turn_four(n, carry):
        for u in range(4):
            turn(4 * n + u, carry)
        return carry
    lax.fori_loop(0, 16, turn_four, 0)

    @pl.when(half == 0)
    def _():
        peers(lambda peer: remote(
            kv_send.at[0], kv_recv.at[peer], kv_ssem.at[0], kv_rsem.at[peer], peer).wait_recv())
    peers(lambda peer: remote(
        q_send.at[peer], q_recv.at[peer], q_ssem.at[peer], q_rsem.at[peer], peer).wait_recv())
    for i in range(GR):
        q_sum = (q_recv[4 * i] + q_recv[4 * i + 1]) + (q_recv[4 * i + 2] + q_recv[4 * i + 3])
        for s in range(2):
            queries[:, s * GR + i, :] = q_sum[:, s * HD:(s + 1) * HD]
    kv_new = jnp.sum(kv_recv[...], axis=0).astype(bf16).astype(f32)
    key_load.wait()
    value_load.wait()
    scale = 1.0 / HD**0.5
    positions = lax.broadcasted_iota(jnp.int32, (8, key_ref.shape[1]), 1)
    for b in range(ROWS):
        q_b = queries[b].astype(bf16)
        scores = lax.dot_general(q_b, key_ref[b], contract, preferred_element_type=f32) * scale
        masked = positions < lengths_ref[0, b]
        scores = jnp.where(masked, scores, -1e30)
        new_score = jnp.sum(
            q_b.astype(f32) * kv_new[b:b + 1, :HD], axis=-1, keepdims=True) * scale
        new_score = jnp.where(half == 0, new_score, -1e30)
        top = jnp.maximum(jnp.max(scores, axis=-1, keepdims=True), new_score)
        weights = jnp.where(masked, jnp.exp(scores - top), 0.0)
        new_weight = jnp.exp(new_score - top)
        total = jnp.sum(weights, axis=-1, keepdims=True) + new_weight
        summed = jnp.dot(weights.astype(bf16), value_ref[b], preferred_element_type=f32)
        summed = summed + new_weight.astype(bf16).astype(f32) * kv_new[b:b + 1, HD:]
        stats[b, 0] = summed
        stats[b, 1] = jnp.broadcast_to(top, (8, HD))
        stats[b, 2] = jnp.broadcast_to(total, (8, HD))

    st_copy = remote(
        stats.at[pl.ds(4 * (1 - half), 4)], stats_recv, st_ssem, st_rsem, me + 1 - 2 * half)
    st_copy.start()
    st_copy.wait_recv()
    for b in range(4):
        mine = stats[4 * half + b]
        got = stats_recv[b]
        joint = jnp.maximum(mine[1], got[1])
        f_mine = jnp.exp(mine[1] - joint)
        f_got = jnp.exp(got[1] - joint)
        merged = (mine[0] * f_mine + got[0] * f_got) / (mine[2] * f_mine + got[2] * f_got)
        for s in range(2):
            at_send[:, s * 4 + b, :] = merged[s * 4:(s + 1) * 4]

    at_recv[me] = at_send[row]
    peers(lambda peer: remote(
        at_send.at[peer // GR], at_recv.at[me], at_ssem.at[peer], at_rsem.at[me], peer).start())
    peers(lambda peer: remote(
        at_send.at[0], at_recv.at[peer], at_ssem.at[peer], at_rsem.at[peer], peer).wait_recv())

    for g in range(KVH):
        place = jnp.int32(0)
        for m in range(1, KVH):
            place = jnp.where(assign_ref[2 * m] == g, m, place)
        first = at_recv[2 * place]
        second = at_recv[2 * place + 1]
        for s in range(2):
            a = 2 * g + s
            ordered[:, a * HD:(a + 1) * HD] = jnp.concatenate(
                [first[s * 4:(s + 1) * 4], second[s * 4:(s + 1) * 4]], 0).astype(bf16)

    def part_copy(k):
        return remote(
            part_send.at[k], part_recv.at[row], part_ssem.at[k], part_rsem.at[row], GR * col + k)

    for k in range(GR):
        part = lax.dot_general(
            ordered[...], ot_ref[k * 512:(k + 1) * 512, :], contract, preferred_element_type=f32)
        part_send[k] = part

        @pl.when(GR * col + k == me)
        def _(part=part):
            part_recv[row] = part

        pl.when(GR * col + k != me)(lambda k=k: part_copy(k).start())
    for i in range(GR):
        pl.when(GR * i + row != me)(lambda i=i: remote(
            part_send.at[0], part_recv.at[i], part_ssem.at[0], part_rsem.at[i],
            GR * i + row).wait_recv())
    out_ref[0] = (
        (part_recv[0] + part_recv[1]) + (part_recv[2] + part_recv[3])).astype(bf16)

    def drain(peer):
        remote(sq_send.at[0], sq_recv.at[me], sq_ssem.at[peer], sq_rsem.at[me], peer).wait_send()
        remote(q_send.at[peer], q_recv.at[me], q_ssem.at[peer], q_rsem.at[me], peer).wait_send()
        remote(at_send.at[0], at_recv.at[me], at_ssem.at[peer], at_rsem.at[me], peer).wait_send()
    peers(drain)
    for m in range(KVH):
        pl.when(2 * m != me)(lambda m=m: kv_copy(m).wait_send())
    for i in range(GR):
        pl.when(GR * i + row != me)(lambda i=i: x_copy(i).wait_send())
        pl.when(GR * col + i != me)(lambda i=i: part_copy(i).wait_send())
    st_copy.wait_send()


def one_group(
    hidden_in, norm_gain, q_blocks, o_blocks, kv_blocks, kv_assign, key_cache, value_cache, lengths
):
    f32, bf16 = jnp.float32, jnp.bfloat16
    ctx = key_cache.shape[2]
    vmem = pl.BlockSpec(memory_space=pltpu.VMEM)
    smem = pl.BlockSpec(memory_space=pltpu.SMEM)
    hbm = pl.BlockSpec(memory_space=pl.ANY)
    dma = pltpu.SemaphoreType.DMA
    return pl.pallas_call(
        pair_kernel,
        out_shape=jax.ShapeDtypeStruct((1, ROWS, DS), bf16),
        in_specs=[vmem, vmem, smem, smem, hbm, hbm, hbm, hbm, hbm],
        out_specs=vmem,
        scratch_shapes=[
            pltpu.VMEM((2048, 2048), bf16),
            pltpu.VMEM((32768, 128), bf16),
            pltpu.VMEM((2048, 2048), bf16),
            pltpu.VMEM((2, 1024, DS), bf16),
            pltpu.VMEM((ROWS, ctx, HD), bf16),
            pltpu.VMEM((ROWS, ctx, HD), bf16),
            pltpu.VMEM((16, 256), bf16),
            pltpu.VMEM((GR, 16, 256), bf16),
            pltpu.VMEM((1, 1, 128), f32),
            pltpu.VMEM((ROLL, 1, 128), f32),
            pltpu.VMEM((KVH, ROWS, 256), f32),
            pltpu.VMEM((KVH, ROWS, 256), f32),
            pltpu.VMEM((ROLL, ROWS, 256), f32),
            pltpu.VMEM((ROLL, ROWS, 256), f32),
            pltpu.VMEM((KVH, ROWS, 256), f32),
            pltpu.VMEM((ROLL, ROWS, 256), f32),
            pltpu.VMEM((ROWS, 8, HD), f32),
            pltpu.VMEM((ROWS, 3, 8, HD), f32),
            pltpu.VMEM((4, 3, 8, HD), f32),
            pltpu.VMEM((GR, 8, HD), f32),
            pltpu.VMEM((ROLL, 8, HD), f32),
            pltpu.VMEM((ROWS, 2048), bf16),
            pltpu.VMEM((ROWS, 2048), bf16),
            pltpu.VMEM((GR, ROWS, DS), f32),
            pltpu.VMEM((GR, ROWS, DS), f32),
            dma((4,)), dma((KVH,)),
            dma((GR,)), dma((GR,)),
            dma((ROLL,)), dma((ROLL,)),
            dma((ROLL,)), dma((ROLL,)),
            dma((KVH,)), dma((ROLL,)),
            dma, dma,
            dma((ROLL,)), dma((ROLL,)),
            dma((GR,)), dma((GR,)),
        ],
        compiler_params=pltpu.CompilerParams(
            collective_id=0, has_side_effects=True, vmem_limit_bytes=56 * 2**20),
        cost_estimate=pl.CostEstimate(
            flops=2 * 8 * 11 * 2**20, bytes_accessed=26 * 2**20, transcendentals=8 * 8 * ctx),
    )(
        hidden_in, norm_gain.reshape(-1, 128), kv_assign, lengths,
        q_blocks.reshape(2048, 2048), o_blocks.reshape(-1, HD), kv_blocks,
        key_cache[0], value_cache[0],
    )


def solution(mesh):
    return jax.shard_map(
        one_group if mesh.shape["tp"] == ROLL else local,
        mesh=mesh,
        in_specs=(
            P(("groups", "tp"), None, None),
            P(),
            P("tp", None, None, None),
            P("tp", None, None, None),
            P(None, None, "tp"),
            P(),
            P(("groups", "tp"), None, None, None),
            P(("groups", "tp"), None, None, None),
            P(("groups", "tp"), None),
        ),
        out_specs=P(("groups", "tp"), None, None),
        check_vma=False,
    )
```

```python
import jax
import jax.numpy as jnp
from jax import lax
from jax.experimental import pallas as pl
from jax.experimental.pallas import tpu as pltpu
from jax.sharding import PartitionSpec as P

D = 8192
KVH = 8
HD = 128
ROLL = 16
ROWS = 8
GR = 4
QG = 16
DS = 512


def from_partner(value, axis, bit):
    mask = 2**bit
    pairs = [(source, source ^ mask) for source in range(lax.axis_size(axis))]
    return lax.ppermute(value, axis, pairs)


def pick(value, ids, axis):
    slices = [
        lax.dynamic_index_in_dim(value, ids[n], axis, keepdims=True) for n in range(ids.shape[0])
    ]
    return jnp.concatenate(slices, axis)


def norm_rows(rows_float, norm_gain):
    mean_square = jnp.mean(rows_float * rows_float, axis=-1, keepdims=True)
    return (rows_float * lax.rsqrt(mean_square + 1e-05) * norm_gain[None, :]).astype(jnp.bfloat16)


def local(
    hidden_in, norm_gain, q_blocks, o_blocks, kv_blocks, kv_assign, key_cache, value_cache, lengths
):
    ranks = lax.axis_size("tp")
    my_index = lax.axis_index("tp")
    my_rank = my_index % ROLL
    my_half = my_rank % 2
    grid_cols = ranks // GR
    group_count = ranks // ROLL
    col_width = q_blocks.shape[3]
    key_width = kv_blocks.shape[2]
    grid_row = my_index // grid_cols
    grid_col = my_index % grid_cols
    dest_rank = jnp.arange(ROLL, dtype=jnp.int32)
    dest_head = kv_assign
    dest_group = 2 * dest_head + dest_rank % 2
    every_rows = lax.all_gather(hidden_in, "tp", axis=0, tiled=True)
    rows_float = (
        every_rows.reshape(group_count, ROLL, ROWS, DS)
        .transpose(0, 2, 1, 3)
        .reshape(group_count * ROWS, D)
        .astype(jnp.float32)
    )
    normed_every = norm_rows(rows_float, norm_gain)
    col_rows = lax.dynamic_slice_in_dim(normed_every, grid_col * col_width, col_width, 1)
    query_part = jnp.einsum(
        "rc,aec->rae", col_rows, q_blocks[0], preferred_element_type=jnp.float32
    )
    query_part = (
        query_part.reshape(group_count, ROWS, QG, HD)
        .transpose(0, 2, 1, 3)
    )
    query_pick = pick(query_part, dest_group, 1).reshape(ranks, ROWS, HD)
    slot_mask = (jnp.arange(GR, dtype=jnp.int32) == grid_row).astype(jnp.float32)
    query_term = (query_pick[:, :, None, :] * slot_mask[None, None, :, None]).reshape(
        ranks, ROWS, GR * HD
    )
    key_rows = lax.dynamic_slice_in_dim(normed_every, my_index * key_width, key_width, 1)
    keyval_part = jnp.einsum("rc,kfc->rkf", key_rows, kv_blocks, preferred_element_type=jnp.float32)
    keyval_part = (
        keyval_part.reshape(group_count, ROWS, 2, KVH, HD)
        .transpose(0, 3, 1, 2, 4)
        .reshape(group_count, KVH, ROWS, 2 * HD)
    )
    keyval_term = pick(keyval_part, dest_head, 1).reshape(ranks, ROWS, 2 * HD)
    proj_term = jnp.concatenate([query_term, keyval_term], -1).reshape(ranks * ROWS, (GR + 2) * HD)
    projected = lax.psum_scatter(proj_term, "tp", scatter_dimension=0, tiled=True)
    queries = projected[:, : GR * HD].astype(jnp.bfloat16)
    keyval_new = projected[:, GR * HD :].astype(jnp.bfloat16)
    key_new = keyval_new[:, :HD]
    value_new = keyval_new[:, HD:]
    partner_queries = from_partner(queries, "tp", 0)
    both_queries = jnp.where(
        my_half == 0,
        jnp.concatenate([queries, partner_queries], 1),
        jnp.concatenate([partner_queries, queries], 1),
    )
    both_queries = both_queries.reshape(ROWS, 2 * GR, HD)
    scale = 1.0 / HD**0.5
    scores = (
        jnp.einsum("bhe,bte->bht", both_queries, key_cache[0], preferred_element_type=jnp.float32)
        * scale
    )
    positions = jnp.arange(scores.shape[2], dtype=jnp.int32)
    masked = positions[None, None, :] < lengths[0][:, None, None]
    new_score = (
        jnp.einsum("bhe,be->bh", both_queries, key_new, preferred_element_type=jnp.float32) * scale
    )
    new_score = jnp.where(my_half == 0, new_score, jnp.float32(-1e30))
    top = jnp.maximum(jnp.max(jnp.where(masked, scores, jnp.float32(-1e30)), axis=-1), new_score)
    weights = jnp.where(masked, jnp.exp(scores - top[..., None]), jnp.float32(0.0))
    new_weight = jnp.exp(new_score - top)
    total = jnp.sum(weights, axis=-1) + new_weight
    summed = jnp.einsum(
        "bht,bte->bhe",
        weights.astype(jnp.bfloat16),
        value_cache[0],
        preferred_element_type=jnp.float32,
    )
    new_rounded = lax.optimization_barrier(new_weight.astype(jnp.bfloat16)).astype(jnp.float32)
    summed = summed + new_rounded[..., None] * value_new.astype(jnp.float32)[:, None, :]
    top_split = top.reshape(ROWS, 2, GR)
    total_split = total.reshape(ROWS, 2, GR)
    summed_split = summed.reshape(ROWS, 2, GR, HD)
    first_half = my_half == 0
    own_top = jnp.where(first_half, top_split[:, 0], top_split[:, 1])
    own_total = jnp.where(first_half, total_split[:, 0], total_split[:, 1])
    own_summed = jnp.where(first_half, summed_split[:, 0], summed_split[:, 1])
    give_top = jnp.where(first_half, top_split[:, 1], top_split[:, 0])
    give_total = jnp.where(first_half, total_split[:, 1], total_split[:, 0])
    give_summed = jnp.where(first_half, summed_split[:, 1], summed_split[:, 0])
    got_top, got_total, got_summed = from_partner((give_top, give_total, give_summed), "tp", 0)
    joint = jnp.maximum(own_top, got_top)
    factor_own = jnp.exp(own_top - joint)
    factor_got = jnp.exp(got_top - joint)
    numer = own_summed * factor_own[..., None] + got_summed * factor_got[..., None]
    denom = own_total * factor_own + got_total * factor_got
    attention = (numer / denom[..., None]).astype(jnp.bfloat16).reshape(ROWS, GR * HD)
    every_attn = lax.all_gather(attention[None], "tp", axis=0, tiled=True)
    head_ids = jnp.arange(KVH, dtype=jnp.int32)
    pair_heads = kv_assign[0::2]
    inverse = jnp.sum(
        head_ids[None, :] * (pair_heads[None, :] == head_ids[:, None]).astype(jnp.int32), axis=1
    )
    slot_ids = jnp.arange(QG, dtype=jnp.int32)
    rank_of_slot = 2 * inverse[slot_ids // 2] + slot_ids % 2
    attn_grid = every_attn.reshape(group_count, ROLL, ROWS, GR, HD)
    row_slot = lax.dynamic_index_in_dim(attn_grid, grid_row, 3, keepdims=False)
    chosen = pick(row_slot, rank_of_slot, 1)
    out_part = jnp.einsum("gabe,cae->gbc", chosen, o_blocks[0], preferred_element_type=jnp.float32)
    placed = jnp.zeros((group_count, ROWS, D), jnp.float32)
    placed = lax.dynamic_update_slice_in_dim(placed, out_part, grid_col * col_width, 2)
    out_term = (
        placed.reshape(group_count, ROWS, ROLL, DS).transpose(0, 2, 1, 3).reshape(ranks * ROWS, DS)
    )
    my_cols = lax.psum_scatter(out_term, "tp", scatter_dimension=0, tiled=True)
    return my_cols.astype(jnp.bfloat16)[None]


def pair_kernel(
    hidden_ref, gain_ref, assign_ref, lengths_ref, q_hbm, o_hbm, kv_hbm, key_hbm, value_hbm,
    out_ref,
    q_ref, o_ref, ot_ref, kv_ref, key_ref, value_ref,
    x_send, x_recv, sq_send, sq_recv, qpart, kvpart, q_send, q_recv, kv_send, kv_recv,
    queries, stats, stats_recv, at_send, at_recv, normed, ordered, part_send, part_recv,
    load_sem, qload_sem, x_ssem, x_rsem, sq_ssem, sq_rsem, q_ssem, q_rsem, kv_ssem, kv_rsem,
    st_ssem, st_rsem, at_ssem, at_rsem, part_ssem, part_rsem,
):
    me = lax.axis_index("tp")
    row = me // GR
    col = me % GR
    half = me % 2
    bf16 = jnp.bfloat16
    f32 = jnp.float32

    def remote(src, dst, send, recv, dest):
        return pltpu.make_async_remote_copy(
            src_ref=src, dst_ref=dst, send_sem=send, recv_sem=recv,
            device_id={"tp": dest}, device_id_type=pl.DeviceIdType.MESH,
        )

    def peers(body):
        def step(p, carry):
            for u in range(1, 6):
                body(lax.rem(me + 5 * p + u, ROLL))
            return carry
        lax.fori_loop(0, (ROLL - 1) // 5, step, 0)

    barrier = pltpu.get_barrier_semaphore()
    peers(lambda peer: pl.semaphore_signal(
        barrier, inc=1, device_id={"tp": peer}, device_id_type=pl.DeviceIdType.MESH))

    kv_load = pltpu.make_async_copy(kv_hbm, kv_ref, load_sem.at[0])
    kv_load.start()
    q_loads = []
    for n in range(KVH):
        span = pl.ds(n * 256, 256)
        q_loads.append(pltpu.make_async_copy(q_hbm.at[span], q_ref.at[span], qload_sem.at[n]))
        q_loads[n].start()

    own = hidden_ref[0].astype(f32)
    packed = jnp.concatenate([own[:, :256], own[:, 256:]], 0).astype(bf16)
    x_send[...] = packed
    squares = jnp.sum(own * own, axis=-1, keepdims=True)
    diagonal = lax.broadcasted_iota(jnp.int32, (ROWS, 128), 0) == lax.broadcasted_iota(
        jnp.int32, (ROWS, 128), 1)
    sq_row = jnp.sum(jnp.where(diagonal, squares, 0.0), axis=0, keepdims=True)
    sq_send[0] = sq_row
    sq_recv[me] = sq_row

    @pl.when(row == col)
    def _():
        x_recv[col] = packed

    @pl.when(half == 1)
    def _():
        kv_recv[...] = jnp.zeros_like(kv_recv)

    pl.semaphore_wait(barrier, ROLL - 1)
    peers(lambda peer: remote(
        sq_send.at[0], sq_recv.at[me], sq_ssem.at[peer], sq_rsem.at[me], peer).start())

    def x_copy(i):
        return remote(x_send, x_recv.at[col], x_ssem.at[i], x_rsem.at[col], GR * i + row)

    for i in range(GR):
        pl.when(GR * i + row != me)(lambda i=i: x_copy(i).start())

    o_load = pltpu.make_async_copy(o_hbm, o_ref, load_sem.at[1])
    key_load = pltpu.make_async_copy(key_hbm, key_ref, load_sem.at[2])
    value_load = pltpu.make_async_copy(value_hbm, value_ref, load_sem.at[3])
    o_load.start()
    key_load.start()
    value_load.start()

    peers(lambda peer: remote(
        sq_send.at[0], sq_recv.at[peer], sq_ssem.at[peer], sq_rsem.at[peer], peer).wait_recv())
    total_sq = jnp.sum(sq_recv[...], axis=0)
    mean_sq = jnp.sum(jnp.where(diagonal, total_sq, 0.0), axis=-1, keepdims=True) * (1.0 / D)
    inv_root = lax.rsqrt(mean_sq + 1e-05)

    own_normed = jnp.concatenate([
        own[:, t * 128:(t + 1) * 128] * inv_root * gain_ref[pl.ds(me * 4 + t, 1), :]
        for t in range(4)], 1).astype(bf16)
    kv_load.wait()
    contract = (((1,), (1,)), ((), ()))
    for c in range(2):
        made = lax.dot_general(own_normed, kv_ref[c], contract, preferred_element_type=f32)
        for g in range(KVH):
            kvpart[g, :, c * HD:(c + 1) * HD] = made[:, g * HD:(g + 1) * HD]

    def kv_copy(m):
        return remote(
            kv_send.at[m], kv_recv.at[me], kv_ssem.at[m], kv_rsem.at[me], 2 * m)

    def kv_step(m, carry):
        term = kvpart[assign_ref[2 * m]]
        kv_send[m] = term

        @pl.when(2 * m == me)
        def _():
            kv_recv[me] = term

        pl.when(2 * m != me)(lambda: kv_copy(m).start())
        return carry
    lax.fori_loop(0, KVH, kv_step, 0)

    for k in range(GR):
        pl.when(GR * col + k != me)(lambda k=k: remote(
            x_send, x_recv.at[k], x_ssem.at[k], x_rsem.at[k], GR * col + k).wait_recv())
        block = x_recv[k].astype(f32)
        for t in range(4):
            lo = (t % 2) * 128
            tile = block[(t // 2) * ROWS:(t // 2 + 1) * ROWS, lo:lo + 128]
            gain = gain_ref[pl.ds(16 * col + 4 * k + t, 1), :]
            at = k * 512 + t * 128
            normed[:, at:at + 128] = (tile * inv_root * gain).astype(bf16)
    for n in range(KVH):
        q_loads[n].wait()
        qpart[n] = lax.dot_general(
            normed[...], q_ref[n * 256:(n + 1) * 256, :], contract, preferred_element_type=f32)

    q_own = qpart[assign_ref[me]]
    q_recv[me] = q_own

    def q_start(peer):
        q_send[peer] = qpart[assign_ref[peer]]
        remote(q_send.at[peer], q_recv.at[me], q_ssem.at[peer], q_rsem.at[me], peer).start()
    peers(q_start)

    o_load.wait()
    r_ids = lax.broadcasted_iota(jnp.int32, (256, 256), 0)
    c_ids = lax.broadcasted_iota(jnp.int32, (256, 256), 1)
    shuffle = jnp.where(c_ids == (r_ids % 16) * 16 + r_ids // 16, 1.0, 0.0).astype(bf16)

    def turn(n, carry):
        base = pl.multiple_of(n * 512, 512)
        rhs = jnp.concatenate(
            [o_ref[pl.ds(base, 256), :], o_ref[pl.ds(base + 256, 256), :]], 1)
        turned = jnp.dot(shuffle, rhs, preferred_element_type=f32).astype(bf16)
        to = pl.multiple_of(n * 32, 32)
        for a in range(QG):
            for u in range(2):
                ot_ref[pl.ds(to + 16 * u, 16), a * HD:(a + 1) * HD] = turned[
                    a * 16:(a + 1) * 16, u * 128:(u + 1) * 128]
        return carry

    def turn_four(n, carry):
        for u in range(4):
            turn(4 * n + u, carry)
        return carry
    lax.fori_loop(0, 16, turn_four, 0)

    @pl.when(half == 0)
    def _():
        peers(lambda peer: remote(
            kv_send.at[0], kv_recv.at[peer], kv_ssem.at[0], kv_rsem.at[peer], peer).wait_recv())
    peers(lambda peer: remote(
        q_send.at[peer], q_recv.at[peer], q_ssem.at[peer], q_rsem.at[peer], peer).wait_recv())
    for i in range(GR):
        q_sum = (q_recv[4 * i] + q_recv[4 * i + 1]) + (q_recv[4 * i + 2] + q_recv[4 * i + 3])
        for s in range(2):
            queries[:, s * GR + i, :] = q_sum[:, s * HD:(s + 1) * HD]
    kv_new = jnp.sum(kv_recv[...], axis=0).astype(bf16).astype(f32)
    key_load.wait()
    value_load.wait()
    scale = 1.0 / HD**0.5
    positions = lax.broadcasted_iota(jnp.int32, (8, key_ref.shape[1]), 1)
    for b in range(ROWS):
        q_b = queries[b].astype(bf16)
        scores = lax.dot_general(q_b, key_ref[b], contract, preferred_element_type=f32) * scale
        masked = positions < lengths_ref[0, b]
        scores = jnp.where(masked, scores, -1e30)
        new_score = jnp.sum(
            q_b.astype(f32) * kv_new[b:b + 1, :HD], axis=-1, keepdims=True) * scale
        new_score = jnp.where(half == 0, new_score, -1e30)
        top = jnp.maximum(jnp.max(scores, axis=-1, keepdims=True), new_score)
        weights = jnp.where(masked, jnp.exp(scores - top), 0.0)
        new_weight = jnp.exp(new_score - top)
        total = jnp.sum(weights, axis=-1, keepdims=True) + new_weight
        summed = jnp.dot(weights.astype(bf16), value_ref[b], preferred_element_type=f32)
        summed = summed + new_weight.astype(bf16).astype(f32) * kv_new[b:b + 1, HD:]
        stats[b, 0] = summed
        stats[b, 1] = jnp.broadcast_to(top, (8, HD))
        stats[b, 2] = jnp.broadcast_to(total, (8, HD))

    st_copy = remote(
        stats.at[pl.ds(4 * (1 - half), 4)], stats_recv, st_ssem, st_rsem, me + 1 - 2 * half)
    st_copy.start()
    st_copy.wait_recv()
    for b in range(4):
        mine = stats[4 * half + b]
        got = stats_recv[b]
        joint = jnp.maximum(mine[1], got[1])
        f_mine = jnp.exp(mine[1] - joint)
        f_got = jnp.exp(got[1] - joint)
        merged = (mine[0] * f_mine + got[0] * f_got) / (mine[2] * f_mine + got[2] * f_got)
        for s in range(2):
            at_send[:, s * 4 + b, :] = merged[s * 4:(s + 1) * 4]

    at_recv[me] = at_send[row]
    peers(lambda peer: remote(
        at_send.at[peer // GR], at_recv.at[me], at_ssem.at[peer], at_rsem.at[me], peer).start())
    peers(lambda peer: remote(
        at_send.at[0], at_recv.at[peer], at_ssem.at[peer], at_rsem.at[peer], peer).wait_recv())

    for g in range(KVH):
        place = jnp.int32(0)
        for m in range(1, KVH):
            place = jnp.where(assign_ref[2 * m] == g, m, place)
        first = at_recv[2 * place]
        second = at_recv[2 * place + 1]
        for s in range(2):
            a = 2 * g + s
            ordered[:, a * HD:(a + 1) * HD] = jnp.concatenate(
                [first[s * 4:(s + 1) * 4], second[s * 4:(s + 1) * 4]], 0).astype(bf16)

    def part_copy(k):
        return remote(
            part_send.at[k], part_recv.at[row], part_ssem.at[k], part_rsem.at[row], GR * col + k)

    for k in range(GR):
        part = lax.dot_general(
            ordered[...], ot_ref[k * 512:(k + 1) * 512, :], contract, preferred_element_type=f32)
        part_send[k] = part

        @pl.when(GR * col + k == me)
        def _(part=part):
            part_recv[row] = part

        pl.when(GR * col + k != me)(lambda k=k: part_copy(k).start())
    for i in range(GR):
        pl.when(GR * i + row != me)(lambda i=i: remote(
            part_send.at[0], part_recv.at[i], part_ssem.at[0], part_rsem.at[i],
            GR * i + row).wait_recv())
    out_ref[0] = (
        (part_recv[0] + part_recv[1]) + (part_recv[2] + part_recv[3])).astype(bf16)

    def drain(peer):
        remote(sq_send.at[0], sq_recv.at[me], sq_ssem.at[peer], sq_rsem.at[me], peer).wait_send()
        remote(q_send.at[peer], q_recv.at[me], q_ssem.at[peer], q_rsem.at[me], peer).wait_send()
        remote(at_send.at[0], at_recv.at[me], at_ssem.at[peer], at_rsem.at[me], peer).wait_send()
    peers(drain)
    for m in range(KVH):
        pl.when(2 * m != me)(lambda m=m: kv_copy(m).wait_send())
    for i in range(GR):
        pl.when(GR * i + row != me)(lambda i=i: x_copy(i).wait_send())
        pl.when(GR * col + i != me)(lambda i=i: part_copy(i).wait_send())
    st_copy.wait_send()


def one_group(
    hidden_in, norm_gain, q_blocks, o_blocks, kv_blocks, kv_assign, key_cache, value_cache, lengths
):
    f32, bf16 = jnp.float32, jnp.bfloat16
    ctx = key_cache.shape[2]
    vmem = pl.BlockSpec(memory_space=pltpu.VMEM)
    smem = pl.BlockSpec(memory_space=pltpu.SMEM)
    hbm = pl.BlockSpec(memory_space=pl.ANY)
    dma = pltpu.SemaphoreType.DMA
    return pl.pallas_call(
        pair_kernel,
        out_shape=jax.ShapeDtypeStruct((1, ROWS, DS), bf16),
        in_specs=[vmem, vmem, smem, smem, hbm, hbm, hbm, hbm, hbm],
        out_specs=vmem,
        scratch_shapes=[
            pltpu.VMEM((2048, 2048), bf16),
            pltpu.VMEM((32768, 128), bf16),
            pltpu.VMEM((2048, 2048), bf16),
            pltpu.VMEM((2, 1024, DS), bf16),
            pltpu.VMEM((ROWS, ctx, HD), bf16),
            pltpu.VMEM((ROWS, ctx, HD), bf16),
            pltpu.VMEM((16, 256), bf16),
            pltpu.VMEM((GR, 16, 256), bf16),
            pltpu.VMEM((1, 1, 128), f32),
            pltpu.VMEM((ROLL, 1, 128), f32),
            pltpu.VMEM((KVH, ROWS, 256), f32),
            pltpu.VMEM((KVH, ROWS, 256), f32),
            pltpu.VMEM((ROLL, ROWS, 256), f32),
            pltpu.VMEM((ROLL, ROWS, 256), f32),
            pltpu.VMEM((KVH, ROWS, 256), f32),
            pltpu.VMEM((ROLL, ROWS, 256), f32),
            pltpu.VMEM((ROWS, 8, HD), f32),
            pltpu.VMEM((ROWS, 3, 8, HD), f32),
            pltpu.VMEM((4, 3, 8, HD), f32),
            pltpu.VMEM((GR, 8, HD), f32),
            pltpu.VMEM((ROLL, 8, HD), f32),
            pltpu.VMEM((ROWS, 2048), bf16),
            pltpu.VMEM((ROWS, 2048), bf16),
            pltpu.VMEM((GR, ROWS, DS), f32),
            pltpu.VMEM((GR, ROWS, DS), f32),
            dma((4,)), dma((KVH,)),
            dma((GR,)), dma((GR,)),
            dma((ROLL,)), dma((ROLL,)),
            dma((ROLL,)), dma((ROLL,)),
            dma((KVH,)), dma((ROLL,)),
            dma, dma,
            dma((ROLL,)), dma((ROLL,)),
            dma((GR,)), dma((GR,)),
        ],
        compiler_params=pltpu.CompilerParams(
            collective_id=0, has_side_effects=True, vmem_limit_bytes=56 * 2**20),
        cost_estimate=pl.CostEstimate(
            flops=2 * 8 * 11 * 2**20, bytes_accessed=26 * 2**20, transcendentals=8 * 8 * ctx),
    )(
        hidden_in, norm_gain.reshape(-1, 128), kv_assign, lengths,
        q_blocks.reshape(2048, 2048), o_blocks.reshape(-1, HD), kv_blocks,
        key_cache[0], value_cache[0],
    )


def solution(mesh):
    return jax.shard_map(
        one_group if mesh.shape["tp"] == ROLL else local,
        mesh=mesh,
        in_specs=(
            P(("groups", "tp"), None, None),
            P(),
            P("tp", None, None, None),
            P("tp", None, None, None),
            P(None, None, "tp"),
            P(),
            P(("groups", "tp"), None, None, None),
            P(("groups", "tp"), None, None, None),
            P(("groups", "tp"), None),
        ),
        out_specs=P(("groups", "tp"), None, None),
        check_vma=False,
    )
```
